32 devices in a mesh: groups: 2 (over x), dev: 16 (over z, y, core).
Axes of the slice: x: 2, y: 2, z: 4, core: 2. Of those that a mesh axis runs over, the one named last changes fastest.
Arguments:
- tokens: bfloat16 [5888, 4096], P(('groups', 'dev')), parts along dimension 0, may hold values from -6 to 6
- output_cotangent: bfloat16 [5888, 1024], P(('groups', 'dev')), parts along dimension 0, may hold values from -6 to 6
- frozen_value_weight: bfloat16 [4096, 1024], replicated, may hold values from -0.09375 to 0.09375
- tenant_down_factor: bfloat16 [128, 4096, 16], P(('groups', 'dev')), parts along dimension 0, may hold values from -0.09375 to 0.09375
- tenant_up_factor: bfloat16 [128, 16, 1024], P(('groups', 'dev')), parts along dimension 0, may hold values from -1.5 to 1.5
- token_owner_device: int32 [5888, 1], P(('groups', 'dev')), parts along dimension 0, may hold values from 0 to 15; in each aligned block of 184 rows (0 to 183, 184 to 367, ...) at most 23 rows name the same one
- token_adapter_slot: int32 [5888], P(('groups', 'dev')), parts along dimension 0, may hold values from 0 to 3
Outputs:
- layer_out: bfloat16 [5888, 1024], P(('groups', 'dev')), parts along dimension 0
- grad_tokens: bfloat16 [5888, 4096], P(('groups', 'dev')), parts along dimension 0
- grad_a: bfloat16 [128, 4096, 16], P(('groups', 'dev')), parts along dimension 0
- up_factor_gradient: bfloat16 [128, 16, 1024], P(('groups', 'dev')), parts along dimension 0
The draws below stay inside these ranges and needn't reach their ends.
There are 2 independent parts, one for each index of `groups`. The reference program is written for one: setup_inputs(seed, part) draws one part's arguments, and reference() takes and returns one part's arrays. A program takes and returns all parts, laid end to end along the dimension named above; an argument that names none is the same for every part. Nothing has to cross between parts.
Inputs may be any that keep to these rules, and one draw needn't show every extreme that they name: `token_owner_device`: in the tokens of one device no owner is named more than 23 times, a bound that some block reaches.
All inputs are finite; a program needn't handle non-finite values.
Results may differ from the reference program's by a relative error of at most 0.0055.
Values may be sent and summed in bfloat16 or wider, within the bound.
A program may use at most 128 MiB of HBM per device.

```python
import math
import jax
import jax.numpy as jnp
import numpy as np
from jax import lax

MODEL_DIM = 4096
VALUE_OUTPUTS = 1024
ADAPTER_RANK = 16
TEN_DEV = 4
TOK_DEV = 184
TENANT_TOTAL = 64
TOKENS = 2944
CAP = 23
N_DEV = 16


def with_ends(values, stream_key, low, top_value):
    index_at = [jax.random.randint(jax.random.fold_in(stream_key, axis), (), 0, length) for axis, length in enumerate(values.shape)]
    main_axis = values.shape.index(max(values.shape))
    neighbour = index_at[:main_axis] + [(index_at[main_axis] + 1) % values.shape[main_axis]] + index_at[main_axis + 1:]
    return values.at[tuple(index_at)].set(low).at[tuple(neighbour)].set(top_value)


def steps_of(key, shape, shards, low, top_value):
    def one(axis_at, parts):
        draws = jax.random.uniform(jax.random.fold_in(jax.random.fold_in(key, 6), axis_at), (parts,), jnp.float32, low / len(shards), top_value / len(shards))
        return jnp.repeat(jnp.exp(draws), shape[axis_at] // parts).reshape((-1,) + (1,) * (len(shape) - axis_at - 1))

    gain = one(*shards[0])
    for cut in shards[1:]:
        gain = gain * one(*cut)
    return gain


def assign_block(stream_key, own, number, rows, number_of, top, limit, lean):
    sequence = jax.random.permutation(stream_key, number_of)
    crowded, common = portions_of(number_of, rows * top, limit, lean, True), portions_of(number_of, rows * top, limit, lean, False)
    places = jnp.arange(number_of)

    def named(lengths, rotation):
        used = int((lengths > 0).sum())
        fixed = max(1, used // 4)
        shifted = fixed + (places - fixed + rotation * (used - fixed)) % max(1, number_of - fixed)
        return jnp.zeros((number_of,), jnp.int32).at[sequence[jnp.where(places < fixed, places, shifted)]].set(jnp.asarray(lengths, jnp.int32))

    lengths = jnp.where(number % 4 == 0, named(crowded, number // 4), named(common, number - number // 4 - 1))
    mixed = jax.random.permutation(jax.random.fold_in(own, 3), number_of)
    source_of, taker = mixed[0:number_of // 2 * 2:2], mixed[1:number_of // 2 * 2:2]
    margin = jnp.minimum(lengths[source_of] - 1, limit - lengths[taker]) // 2
    margin = jnp.where((source_of == sequence[0]) | (taker == sequence[0]) | (lengths[taker] == 0), 0, jnp.maximum(margin, 0))
    shifted = jax.random.randint(jax.random.fold_in(own, 4), (number_of // 2,), 0, 1 << 20) % (margin + 1)
    lengths = lengths.at[source_of].add(-shifted).at[taker].add(shifted)
    items = jnp.searchsorted(jnp.cumsum(lengths), jnp.arange(rows * top), side="right").astype(jnp.int32)
    grid = items.reshape(top, rows).T
    grid = grid[jax.random.permutation(jax.random.fold_in(own, 1), rows)]
    rotation = jax.random.randint(jax.random.fold_in(own, 2), (rows, 1), 0, top)
    return jnp.take_along_axis(grid, (jnp.arange(top)[None, :] + rotation) % top, axis=1)


def portions_of(number_of, total, bound, lean, full):
    portions = [(1 << 20) // math.isqrt(grade ** lean) + 1 for grade in range(1, number_of + 1)]
    largest = bound if full else min(bound, max(-(-total // number_of), total * portions[0] // sum(portions)))
    least = 1 if total - largest >= number_of - 1 else 0
    holding, spare = [largest] + [least] * (number_of - 1), total - largest - least * (number_of - 1)
    while spare > 0:
        candidates = [i for i in range(1, number_of) if holding[i] < largest] or [i for i in range(1, number_of) if holding[i] < bound]
        pool, budget = sum([portions[i] for i in candidates]), spare
        for i in candidates:
            extra = min(bound - holding[i], max(1, budget * portions[i] // pool), spare)
            holding[i] = holding[i] + extra
            spare = spare - extra
    return np.array(holding)


def scatter_about(rng, shape, width, reach, cuts=(), held_as=jnp.bfloat16):
    values = jax.random.normal(rng, shape, jnp.float32) * width
    if len(cuts) > 0:
        values = steps_of(rng, shape, cuts, -0.22, 0.18) * values
    return jnp.clip(values, min=-reach, max=reach).astype(held_as)


def setup_inputs(seed: int = 0, part: int = 0) -> dict:
    arg_keys = jax.random.split(jax.random.key(seed), 8)
    part_keys = jax.random.split(jax.random.fold_in(arg_keys[7], part), 8)
    tokens = scatter_about(part_keys[0], (TOKENS, MODEL_DIM), 1.0, 6.0, ((0, 16),))
    output_cotangent = scatter_about(part_keys[1], (TOKENS, VALUE_OUTPUTS), 1.0, 6.0, ((0, 16),))
    frozen_value_weight = scatter_about(arg_keys[2], (MODEL_DIM, VALUE_OUTPUTS), MODEL_DIM ** -0.5, 0.09375)
    tenant_down_factor = scatter_about(part_keys[3], (TENANT_TOTAL, MODEL_DIM, ADAPTER_RANK), MODEL_DIM ** -0.5, 0.09375, ((0, 16),))
    tenant_up_factor = scatter_about(part_keys[4], (TENANT_TOTAL, ADAPTER_RANK, VALUE_OUTPUTS), ADAPTER_RANK ** -0.5, 1.5, ((0, 16),))
    token_owner_device_keys = jax.random.split(jax.random.fold_in(part_keys[5], 1), TOKENS // TOK_DEV)
    token_owner_device_turns = jax.random.permutation(jax.random.fold_in(part_keys[5], 3), TOKENS // TOK_DEV)
    token_owner_device = jax.vmap(lambda own, number: assign_block(jax.random.fold_in(part_keys[5], 2), own, number, TOK_DEV, N_DEV, 1, CAP, 2))(token_owner_device_keys, token_owner_device_turns).reshape((TOKENS, 1))
    token_adapter_slot = with_ends(jax.random.randint(part_keys[6], (TOKENS,), 0, TEN_DEV), jax.random.fold_in(part_keys[6], 1), 0, TEN_DEV - 1).astype(jnp.int32)
    return {"tokens": tokens, "output_cotangent": output_cotangent, "frozen_value_weight": frozen_value_weight, "tenant_down_factor": tenant_down_factor, "tenant_up_factor": tenant_up_factor, "token_owner_device": token_owner_device, "token_adapter_slot": token_adapter_slot}


adapter_scale = 2.0

def reference(tokens, output_cotangent, frozen_value_weight, tenant_down_factor, tenant_up_factor, token_owner_device, token_adapter_slot):
    tenant_ids = (token_owner_device[:, 0] * TEN_DEV + token_adapter_slot).astype(jnp.int32)
    token_blocks = tokens.reshape(N_DEV, TOK_DEV, MODEL_DIM)
    grad_blocks = output_cotangent.reshape(N_DEV, TOK_DEV, VALUE_OUTPUTS)
    tenant_blocks = tenant_ids.reshape(N_DEV, TOK_DEV)

    def block_step(carry, block):
        acc_a, acc_b = carry
        x_rows, dy_rows, tenant_labels = block
        down_factor_rows = tenant_down_factor[tenant_labels].astype(jnp.float32)
        up_factor_rows = tenant_up_factor[tenant_labels].astype(jnp.float32)
        input_wide = x_rows.astype(jnp.float32)
        output_grad_wide = dy_rows.astype(jnp.float32)
        projected_rows = jnp.einsum('rd,rdk->rk', input_wide, down_factor_rows).astype(jnp.bfloat16)
        back_rows = jnp.einsum('rv,rkv->rk', output_grad_wide, up_factor_rows).astype(jnp.bfloat16)
        projected_wide = projected_rows.astype(jnp.float32)
        returned_wide = back_rows.astype(jnp.float32)
        adapter_output = (adapter_scale * jnp.einsum('ji,jit->jt', projected_wide, up_factor_rows)).astype(jnp.bfloat16)
        adapter_input_grad = (adapter_scale * jnp.einsum('ma,mga->mg', returned_wide, down_factor_rows)).astype(jnp.bfloat16)
        frozen_output = jnp.dot(x_rows, frozen_value_weight, preferred_element_type=jnp.float32)
        frozen_input_grad = lax.dot_general(dy_rows, frozen_value_weight, (((1,), (1,)), ((), ())), preferred_element_type=jnp.float32)
        output_rows = (frozen_output + adapter_output.astype(jnp.float32)).astype(jnp.bfloat16)
        input_grad_rows = (frozen_input_grad + adapter_input_grad.astype(jnp.float32)).astype(jnp.bfloat16)
        down_outer_product = adapter_scale * input_wide[:, :, None] * returned_wide[:, None, :]
        up_outer_product = adapter_scale * projected_wide[:, :, None] * output_grad_wide[:, None, :]
        acc_a = acc_a + jax.ops.segment_sum(down_outer_product, tenant_labels, num_segments=TENANT_TOTAL)
        acc_b = acc_b + jax.ops.segment_sum(up_outer_product, tenant_labels, num_segments=TENANT_TOTAL)
        return ((acc_a, acc_b), (output_rows, input_grad_rows))
    start = (jnp.zeros((TENANT_TOTAL, MODEL_DIM, ADAPTER_RANK), jnp.float32), jnp.zeros((TENANT_TOTAL, ADAPTER_RANK, VALUE_OUTPUTS), jnp.float32))
    (unclipped_down_grad, unclipped_up_grad), (out_all, dx_all) = lax.scan(block_step, start, (token_blocks, grad_blocks, tenant_blocks))
    norm_value = jnp.sqrt(jnp.sum(unclipped_down_grad * unclipped_down_grad) + jnp.sum(unclipped_up_grad * unclipped_up_grad))
    entry_total = jnp.sqrt(jnp.float32(TENANT_TOTAL * ADAPTER_RANK * (MODEL_DIM + VALUE_OUTPUTS)))
    clipping_scale = jnp.minimum(jnp.float32(1.0), entry_total / (norm_value + 1e-06))
    grad_a = (unclipped_down_grad * clipping_scale).astype(jnp.bfloat16)
    up_factor_gradient = (unclipped_up_grad * clipping_scale).astype(jnp.bfloat16)
    return (out_all.reshape(TOKENS, VALUE_OUTPUTS), dx_all.reshape(TOKENS, MODEL_DIM), grad_a, up_factor_gradient)
```

```python
import jax
import jax.numpy as jnp
from jax import lax
from jax.sharding import PartitionSpec as P

adapter_scale = 2.0
plane = 4
f32 = jnp.float32
bf16 = jnp.bfloat16


def dot_nn(a, b):
    return lax.dot_general(a, b, (((1,), (0,)), ((), ())), preferred_element_type=f32)


def dot_nt(a, b):
    return lax.dot_general(a, b, (((1,), (1,)), ((), ())), preferred_element_type=f32)


def dot_tn(a, b):
    return lax.dot_general(a, b, (((0,), (0,)), ((), ())), preferred_element_type=f32)


def local(x, dy, w, down_f, up_f, owner, slot):
    n = lax.axis_size("dev")
    me = lax.axis_index("dev")
    layers = n // plane
    tenants, hidden, rank = down_f.shape
    width = up_f.shape[2]
    cols = tenants * rank
    columns = [[z * plane + k for z in range(layers)] for k in range(plane)]
    to_core = [(i, i ^ 1) for i in range(n)]
    to_line = [(i, i ^ 2) for i in range(n)]

    def gather(v):
        return lax.all_gather(v, "dev", axis_index_groups=columns, tiled=True)

    def scatter(v):
        return lax.psum_scatter(
            v, "dev", scatter_dimension=0, axis_index_groups=columns, tiled=True
        )

    def swap_core(v):
        return lax.ppermute(v, "dev", to_core)

    def swap_line(v):
        return lax.ppermute(v, "dev", to_line)

    ids = (owner[:, 0] * tenants + slot).reshape(-1, 1)
    ids_p = swap_line(ids)
    up0 = gather(up_f.reshape(cols, width))
    dy_p = swap_line(dy)
    up1 = swap_core(up0)
    down0 = gather(jnp.transpose(down_f, (0, 2, 1)).reshape(cols, hidden))
    x_p = swap_line(x)
    down1 = swap_core(down0)

    col = jnp.arange(layers * cols, dtype=jnp.int32)[None, :]
    label0 = ((col // cols) * plane + me % plane) * tenants + (col // rank) % tenants
    label1 = label0 + jnp.where(me % 2 == 0, tenants, -tenants)
    ids_of = (ids, ids_p)
    keep = [[i == lab for lab in (label0, label1)] for i in ids_of]
    xs, dys, ups, downs = (x, x_p), (dy, dy_p), (up0, up1), (down0, down1)

    def masked(v, k):
        return jnp.where(k, v, 0.0).astype(bf16)

    back = [[masked(dot_nt(dys[r], ups[c]), keep[r][c]) for c in range(2)] for r in range(2)]
    proj = [[masked(dot_nt(xs[r], downs[c]), keep[r][c]) for c in range(2)] for r in range(2)]

    def lora(coef, factors, r):
        return (
            adapter_scale * (dot_nn(coef[r][0], factors[0]) + dot_nn(coef[r][1], factors[1]))
        ).astype(bf16)

    def partial(coef, rows, c):
        return dot_tn(coef[0][c], rows[0]) + dot_tn(coef[1][c], rows[1])

    ga = scatter(
        (partial(back, xs, 0) + swap_core(partial(back, xs, 1).astype(bf16)).astype(f32)).astype(bf16)
    )
    gb = scatter(
        (partial(proj, dys, 0) + swap_core(partial(proj, dys, 1).astype(bf16)).astype(f32)).astype(bf16)
    )
    far_dx = swap_line(lora(back, downs, 1))
    far_y = swap_line(lora(proj, ups, 1))
    near_dx = lora(back, downs, 0)
    near_y = lora(proj, ups, 0)
    layer_out = (dot_nn(x, w) + (near_y.astype(f32) + far_y.astype(f32))).astype(bf16)
    grad_tokens = (dot_nt(dy, w) + (near_dx.astype(f32) + far_dx.astype(f32))).astype(bf16)

    ga = adapter_scale * ga.astype(f32)
    gb = adapter_scale * gb.astype(f32)
    norm = jnp.sqrt(lax.psum(jnp.sum(ga * ga) + jnp.sum(gb * gb), "dev"))
    entries = jnp.sqrt(f32(tenants * n * rank * (hidden + width)))
    factor = jnp.minimum(f32(1.0), entries / (norm + 1e-06))
    grad_a = jnp.transpose((ga * factor).astype(bf16).reshape(tenants, rank, hidden), (0, 2, 1))
    grad_b = (gb * factor).astype(bf16).reshape(tenants, rank, width)
    return (layer_out, grad_tokens, grad_a, grad_b)


def solution(mesh):
    rows = P(("groups", "dev"), None)
    stack = P(("groups", "dev"), None, None)
    return jax.shard_map(
        local,
        mesh=mesh,
        in_specs=(rows, rows, P(), stack, stack, rows, P(("groups", "dev"))),
        out_specs=(rows, rows, stack, stack),
        check_vma=False,
    )
```

```python
import functools

import jax
import jax.numpy as jnp
from jax import lax
from jax.experimental import pallas as pl
from jax.experimental.pallas import tpu as pltpu
from jax.sharding import PartitionSpec as P

adapter_scale = 2.0
plane = 4
f32 = jnp.float32
bf16 = jnp.bfloat16


def dot_nn(a, b):
    return lax.dot_general(a, b, (((1,), (0,)), ((), ())), preferred_element_type=f32)


def dot_nt(a, b):
    return lax.dot_general(a, b, (((1,), (1,)), ((), ())), preferred_element_type=f32)


def dot_tn(a, b):
    return lax.dot_general(a, b, (((0,), (0,)), ((), ())), preferred_element_type=f32)


def long_line(x, dy, w, down_f, up_f, owner, slot):
    n = lax.axis_size("dev")
    me = lax.axis_index("dev")
    layers = n // plane
    tenants, hidden, rank = down_f.shape
    width = up_f.shape[2]
    cols = tenants * rank
    columns = [[z * plane + k for z in range(layers)] for k in range(plane)]
    to_core = [(i, i ^ 1) for i in range(n)]
    to_line = [(i, i ^ 2) for i in range(n)]

    def gather(v):
        return lax.all_gather(v, "dev", axis_index_groups=columns, tiled=True)

    def scatter(v):
        return lax.psum_scatter(
            v, "dev", scatter_dimension=0, axis_index_groups=columns, tiled=True
        )

    def swap_core(v):
        return lax.ppermute(v, "dev", to_core)

    def swap_line(v):
        return lax.ppermute(v, "dev", to_line)

    ids = (owner[:, 0] * tenants + slot).reshape(-1, 1)
    ids_p = swap_line(ids)
    up0 = gather(up_f.reshape(cols, width))
    dy_p = swap_line(dy)
    up1 = swap_core(up0)
    down0 = gather(jnp.transpose(down_f, (0, 2, 1)).reshape(cols, hidden))
    x_p = swap_line(x)
    down1 = swap_core(down0)

    col = jnp.arange(layers * cols, dtype=jnp.int32)[None, :]
    label0 = ((col // cols) * plane + me % plane) * tenants + (col // rank) % tenants
    label1 = label0 + jnp.where(me % 2 == 0, tenants, -tenants)
    ids_of = (ids, ids_p)
    keep = [[i == lab for lab in (label0, label1)] for i in ids_of]
    xs, dys, ups, downs = (x, x_p), (dy, dy_p), (up0, up1), (down0, down1)

    def masked(v, k):
        return jnp.where(k, v, 0.0).astype(bf16)

    back = [[masked(dot_nt(dys[r], ups[c]), keep[r][c]) for c in range(2)] for r in range(2)]
    proj = [[masked(dot_nt(xs[r], downs[c]), keep[r][c]) for c in range(2)] for r in range(2)]

    def lora(coef, factors, r):
        return (
            adapter_scale * (dot_nn(coef[r][0], factors[0]) + dot_nn(coef[r][1], factors[1]))
        ).astype(bf16)

    def partial(coef, rows, c):
        return dot_tn(coef[0][c], rows[0]) + dot_tn(coef[1][c], rows[1])

    ga = scatter(
        (partial(back, xs, 0) + swap_core(partial(back, xs, 1).astype(bf16)).astype(f32)).astype(bf16)
    )
    gb = scatter(
        (partial(proj, dys, 0) + swap_core(partial(proj, dys, 1).astype(bf16)).astype(f32)).astype(bf16)
    )
    far_dx = swap_line(lora(back, downs, 1))
    far_y = swap_line(lora(proj, ups, 1))
    near_dx = lora(back, downs, 0)
    near_y = lora(proj, ups, 0)
    layer_out = (dot_nn(x, w) + (near_y.astype(f32) + far_y.astype(f32))).astype(bf16)
    grad_tokens = (dot_nt(dy, w) + (near_dx.astype(f32) + far_dx.astype(f32))).astype(bf16)

    ga = adapter_scale * ga.astype(f32)
    gb = adapter_scale * gb.astype(f32)
    norm = jnp.sqrt(lax.psum(jnp.sum(ga * ga) + jnp.sum(gb * gb), "dev"))
    entries = jnp.sqrt(f32(tenants * n * rank * (hidden + width)))
    factor = jnp.minimum(f32(1.0), entries / (norm + 1e-06))
    grad_a = jnp.transpose((ga * factor).astype(bf16).reshape(tenants, rank, hidden), (0, 2, 1))
    grad_b = (gb * factor).astype(bf16).reshape(tenants, rank, width)
    return (layer_out, grad_tokens, grad_a, grad_b)


def copy_to(src, dst, send_sem, recv_sem, device):
    return pltpu.make_async_remote_copy(
        src_ref=src,
        dst_ref=dst,
        send_sem=send_sem,
        recv_sem=recv_sem,
        device_id={"dev": device},
        device_id_type=pl.DeviceIdType.MESH,
    )


def greet(barrier, device):
    pl.semaphore_signal(
        barrier, inc=1, device_id={"dev": device}, device_id_type=pl.DeviceIdType.MESH
    )


def position():
    me = lax.axis_index("dev")
    z, core = me // plane, me % 2
    return me, z, core, me + 1 - 2 * core


def gather_kernel(layers, down, up, down_all, up_all, own_sem, send, recv, core_send, core_recv):
    me, z, core, twin = position()
    steps = layers - 1
    arrays = ((down, down_all), (up, up_all))
    inner = z > 0
    outer = z < layers - 1
    barrier = pltpu.get_barrier_semaphore()
    greet(barrier, twin)
    pl.when(inner)(lambda: greet(barrier, me - plane))
    pl.when(outer)(lambda: greet(barrier, me + plane))
    pl.semaphore_wait(barrier, 1 + inner.astype(jnp.int32) + outer.astype(jnp.int32))

    def hop(way, s, a):
        block = z - s if way == 0 else z + s
        own, whole = arrays[a]
        spot = whole.at[block, core]
        k = (way * steps + s) * 2 + a
        target = me + plane if way == 0 else me - plane
        return copy_to(own if s == 0 else spot, spot, send.at[k], recv.at[k], target)

    def landed(way, s, a):
        block = z - 1 - s if way == 0 else z + 1 + s
        own, whole = arrays[a]
        k = (way * steps + s) * 2 + a
        return copy_to(own, whole.at[block, core], send.at[k], recv.at[k], twin)

    def across(way, s, a):
        block = z - 1 - s if way == 0 else z + 1 + s
        spot = arrays[a][1].at[block, core]
        k = (way * steps + s) * 2 + a
        return copy_to(spot, spot, core_send.at[k], core_recv.at[k], twin)

    def from_twin(way, s, a):
        block = z - 1 - s if way == 0 else z + 1 + s
        spot = arrays[a][1].at[block, 1 - core]
        k = (way * steps + s) * 2 + a
        return copy_to(spot, spot, core_send.at[k], core_recv.at[k], twin)

    def sends(way, s):
        return (z >= s) & outer if way == 0 else (z + s <= layers - 1) & inner

    def arrives(way, s):
        return z - 1 - s >= 0 if way == 0 else z + 1 + s <= layers - 1

    def each(copies, act):
        def run():
            for a in range(2):
                act(copies(a))

        return run

    def start(c):
        c.start()

    base = 4 * steps

    def own_across(a):
        return copy_to(
            arrays[a][0],
            arrays[a][1].at[z, core],
            core_send.at[base + a],
            core_recv.at[base + a],
            twin,
        )

    def own_from(a):
        return copy_to(
            arrays[a][0],
            arrays[a][1].at[z, 1 - core],
            core_send.at[base + a],
            core_recv.at[base + a],
            twin,
        )

    def own_copy(a):
        return pltpu.make_async_copy(arrays[a][0], arrays[a][1].at[z, core], own_sem.at[a])

    for s in range(steps):
        for way in range(2):
            pl.when(sends(way, s))(each(functools.partial(hop, way, s), start))
        if s == 0:
            each(own_across, start)()
            each(own_copy, start)()
        for way in range(2):
            pl.when(arrives(way, s))(
                each(functools.partial(landed, way, s), lambda c: c.wait_recv())
            )
        for way in range(2):
            pl.when(arrives(way, s))(each(functools.partial(across, way, s), start))
    for a in range(2):
        own_copy(a).wait()
        own_across(a).wait_send()
        own_from(a).wait_recv()
    for s in range(steps):
        for way in range(2):
            pl.when(sends(way, s))(each(functools.partial(hop, way, s), lambda c: c.wait_send()))
            pl.when(arrives(way, s))(
                each(functools.partial(across, way, s), lambda c: c.wait_send())
            )
            pl.when(arrives(way, s))(
                each(functools.partial(from_twin, way, s), lambda c: c.wait_recv())
            )


def reduce_kernel(
    layers,
    rounds,
    limit,
    part_a,
    part_b,
    out_a,
    out_b,
    twin_a,
    twin_b,
    sum_a,
    sum_b,
    in_a,
    in_b,
    send_a,
    send_b,
    norm_buf,
    twin_send,
    twin_recv,
    hop_send,
    hop_recv,
    norm_send,
    norm_recv,
):
    me, z, core, twin = position()
    inner = z > 0
    outer = z < layers - 1
    arrays = (
        (part_a, twin_a, sum_a, in_a, send_a),
        (part_b, twin_b, sum_b, in_b, send_b),
    )
    partners = []
    for r in range(rounds):
        bit = 2**r
        partners.append(me + bit - 2 * bit * ((me // bit) % 2))
    barrier = pltpu.get_barrier_semaphore()
    for p in partners:
        greet(barrier, p)
    pl.when(inner)(lambda: greet(barrier, me - plane))
    pl.when(outer)(lambda: greet(barrier, me + plane))
    pl.semaphore_wait(barrier, rounds + inner.astype(jnp.int32) + outer.astype(jnp.int32))

    order = []
    for i in range((layers + 1) // 2):
        order += [layers - 1 - i, i] if layers - 1 - i != i else [i]

    def to_twin(j, a):
        part, got = arrays[a][:2]
        k = 2 * j + a
        return copy_to(part.at[j, 1 - core], got.at[j], twin_send.at[k], twin_recv.at[k], twin)

    for j in order:
        for a in range(2):
            to_twin(j, a).start()

    ready = set()

    def prepare(j):
        if j in ready:
            return
        ready.add(j)
        for a in range(2):
            part, got, total = arrays[a][:3]
            to_twin(j, a).wait_recv()
            total[j] = part[j, core].astype(f32) + got[j].astype(f32)

    def hop(way, j, a):
        k = (way * layers + j) * 2 + a
        return copy_to(
            arrays[a][4].at[way, j],
            arrays[a][3].at[way, j],
            hop_send.at[k],
            hop_recv.at[k],
            me + plane if way == 0 else me - plane,
        )

    def take(way, j):
        for a in range(2):
            total, came = arrays[a][2:4]
            hop(way, j, a).wait_recv()
            total[j] = total[j] + came[way, j].astype(f32)

    def forward(way, j):
        pl.when(inner if way == 0 else outer)(lambda: take(way, j))
        for a in range(2):
            total, _, out = arrays[a][2:]
            out[way, j] = total[j].astype(bf16)
            hop(way, j, a).start()

    def moves(way, j):
        return z < j if way == 0 else z > j

    for i in range(layers - 1):
        for way, j in ((0, layers - 1 - i), (1, i)):
            prepare(j)
            pl.when(moves(way, j))(functools.partial(forward, way, j))
    for j in range(layers):
        prepare(j)
    for j in range(layers):
        if j > 0:
            pl.when(z == j)(functools.partial(take, 0, j))
        if j < layers - 1:
            pl.when(z == j)(functools.partial(take, 1, j))

    raw_a = sum_a[z] * adapter_scale
    raw_b = sum_b[z] * adapter_scale
    squares = jnp.sum(raw_a * raw_a) + jnp.sum(raw_b * raw_b)
    norm_buf[0] = jnp.full(norm_buf.shape[1:], squares, f32)
    for r, p in enumerate(partners):
        c = copy_to(norm_buf.at[2 * r], norm_buf.at[2 * r + 1], norm_send.at[r], norm_recv.at[r], p)
        c.start()
        c.wait()
        norm_buf[2 * r + 2] = norm_buf[2 * r] + norm_buf[2 * r + 1]
    norm = jnp.sqrt(norm_buf[2 * rounds][0:1, 0:1])
    factor = jnp.minimum(f32(1.0), f32(limit) / (norm + f32(1e-06)))
    out_a[...] = (sum_a[z] * adapter_scale * factor).astype(bf16)
    out_b[...] = (sum_b[z] * adapter_scale * factor).astype(bf16)

    for j in range(layers):
        for a in range(2):
            to_twin(j, a).wait_send()
        for way in range(2):
            if (way == 0 and j > 0) or (way == 1 and j < layers - 1):

                def settle(way=way, j=j):
                    for a in range(2):
                        hop(way, j, a).wait_send()

                pl.when(moves(way, j))(settle)


def gather_line(layers, down, up):
    cols, hidden = down.shape
    width = up.shape[1]
    sems = 4 * (layers - 1)
    return pl.pallas_call(
        functools.partial(gather_kernel, layers),
        out_shape=(
            jax.ShapeDtypeStruct((layers, 2, cols, hidden), bf16),
            jax.ShapeDtypeStruct((layers, 2, cols, width), bf16),
        ),
        in_specs=[pl.BlockSpec(memory_space=pl.ANY)] * 2,
        out_specs=[pl.BlockSpec(memory_space=pl.ANY)] * 2,
        scratch_shapes=[
            pltpu.SemaphoreType.DMA((2,)),
            pltpu.SemaphoreType.DMA((sems,)),
            pltpu.SemaphoreType.DMA((sems,)),
            pltpu.SemaphoreType.DMA((sems + 2,)),
            pltpu.SemaphoreType.DMA((sems + 2,)),
        ],
        cost_estimate=pl.CostEstimate(flops=0, bytes_accessed=100_000_000, transcendentals=0),
        compiler_params=pltpu.CompilerParams(collective_id=0, has_side_effects=True),
    )(down, up)


def reduce_line(layers, n, limit, part_a, part_b):
    _, _, cols, hidden = part_a.shape
    width = part_b.shape[3]
    rounds = n.bit_length() - 1
    vmem = pl.BlockSpec(memory_space=pltpu.VMEM)

    def both(lead, dtype):
        return [pltpu.VMEM((*lead, cols, m), dtype) for m in (hidden, width)]

    return pl.pallas_call(
        functools.partial(reduce_kernel, layers, rounds, limit),
        out_shape=(
            jax.ShapeDtypeStruct((cols, hidden), bf16),
            jax.ShapeDtypeStruct((cols, width), bf16),
        ),
        in_specs=[vmem] * 2,
        out_specs=[vmem] * 2,
        scratch_shapes=[
            *both((layers,), bf16),
            *both((layers,), f32),
            *both((2, layers), bf16),
            *both((2, layers), bf16),
            pltpu.VMEM((2 * rounds + 1, 8, 128), f32),
            pltpu.SemaphoreType.DMA((2 * layers,)),
            pltpu.SemaphoreType.DMA((2 * layers,)),
            pltpu.SemaphoreType.DMA((4 * layers,)),
            pltpu.SemaphoreType.DMA((4 * layers,)),
            pltpu.SemaphoreType.DMA((rounds,)),
            pltpu.SemaphoreType.DMA((rounds,)),
        ],
        cost_estimate=pl.CostEstimate(flops=0, bytes_accessed=100_000_000, transcendentals=0),
        compiler_params=pltpu.CompilerParams(
            collective_id=1, has_side_effects=True, vmem_limit_bytes=48 * 2**20
        ),
    )(part_a, part_b)


def short_line(x, dy, w, down_f, up_f, owner, slot):
    n = lax.axis_size("dev")
    me = lax.axis_index("dev")
    layers = n // plane
    tenants, hidden, rank = down_f.shape
    width = up_f.shape[2]
    cols = tenants * rank
    to_line = [(i, i ^ 2) for i in range(n)]

    def swap_line(v):
        return lax.ppermute(v, "dev", to_line)

    ids = (owner[:, 0] * tenants + slot).reshape(-1, 1)
    ids_p = swap_line(ids)
    dy_p = swap_line(dy)
    x_p = swap_line(x)
    downs, ups = gather_line(
        layers,
        jnp.transpose(down_f, (0, 2, 1)).reshape(cols, hidden),
        up_f.reshape(cols, width),
    )
    downs = downs.reshape(layers * 2 * cols, hidden)
    ups = ups.reshape(layers * 2 * cols, width)
    frozen_y = dot_nn(x, w)
    frozen_dx = dot_nt(dy, w)

    col = jnp.arange(layers * 2 * cols, dtype=jnp.int32)[None, :]
    device = (col // (2 * cols)) * plane + (me % plane) // 2 * 2 + (col // cols) % 2
    label = device * tenants + (col // rank) % tenants

    def masked(v, i):
        return jnp.where(i == label, v, 0.0).astype(bf16)

    back_p = masked(dot_nt(dy_p, ups), ids_p)
    far_dx = swap_line((adapter_scale * dot_nn(back_p, downs)).astype(bf16))
    proj_p = masked(dot_nt(x_p, downs), ids_p)
    far_y = swap_line((adapter_scale * dot_nn(proj_p, ups)).astype(bf16))
    back = masked(dot_nt(dy, ups), ids)
    proj = masked(dot_nt(x, downs), ids)
    part_a = (dot_tn(back, x) + dot_tn(back_p, x_p)).astype(bf16)
    part_b = (dot_tn(proj, dy) + dot_tn(proj_p, dy_p)).astype(bf16)
    near_dx = (adapter_scale * dot_nn(back, downs)).astype(bf16)
    near_y = (adapter_scale * dot_nn(proj, ups)).astype(bf16)
    limit = float(tenants * n * rank * (hidden + width)) ** 0.5
    grad_a, grad_b = reduce_line(
        layers,
        n,
        limit,
        part_a.reshape(layers, 2, cols, hidden),
        part_b.reshape(layers, 2, cols, width),
    )
    layer_out = (frozen_y + (near_y.astype(f32) + far_y.astype(f32))).astype(bf16)
    grad_tokens = (frozen_dx + (near_dx.astype(f32) + far_dx.astype(f32))).astype(bf16)
    grad_a = jnp.transpose(grad_a.reshape(tenants, rank, hidden), (0, 2, 1))
    return (layer_out, grad_tokens, grad_a, grad_b.reshape(tenants, rank, width))


def local(*args):
    if lax.axis_size("dev") // plane <= 4:
        return short_line(*args)
    return long_line(*args)


def solution(mesh):
    rows = P(("groups", "dev"), None)
    stack = P(("groups", "dev"), None, None)
    return jax.shard_map(
        local,
        mesh=mesh,
        in_specs=(rows, rows, P(), stack, stack, rows, P(("groups", "dev"))),
        out_specs=(rows, rows, stack, stack),
        check_vma=False,
    )
```

```python
import functools

import jax
import jax.numpy as jnp
from jax import lax
from jax.experimental import pallas as pl
from jax.experimental.pallas import tpu as pltpu
from jax.sharding import PartitionSpec as P

adapter_scale = 2.0
piece = 512
plane = 4
f32 = jnp.float32
bf16 = jnp.bfloat16


def dot_nn(a, b):
    return lax.dot_general(a, b, (((1,), (0,)), ((), ())), preferred_element_type=f32)


def dot_nt(a, b):
    return lax.dot_general(a, b, (((1,), (1,)), ((), ())), preferred_element_type=f32)


def dot_tn(a, b):
    return lax.dot_general(a, b, (((0,), (0,)), ((), ())), preferred_element_type=f32)


def long_line(x, dy, w, down_f, up_f, owner, slot):
    n = lax.axis_size("dev")
    me = lax.axis_index("dev")
    layers = n // plane
    tenants, hidden, rank = down_f.shape
    width = up_f.shape[2]
    cols = tenants * rank
    columns = [[z * plane + k for z in range(layers)] for k in range(plane)]
    to_core = [(i, i ^ 1) for i in range(n)]
    to_line = [(i, i ^ 2) for i in range(n)]

    def gather(v):
        return lax.all_gather(v, "dev", axis_index_groups=columns, tiled=True)

    def scatter(v):
        return lax.psum_scatter(
            v, "dev", scatter_dimension=0, axis_index_groups=columns, tiled=True
        )

    def swap_core(v):
        return lax.ppermute(v, "dev", to_core)

    def swap_line(v):
        return lax.ppermute(v, "dev", to_line)

    ids = (owner[:, 0] * tenants + slot).reshape(-1, 1)
    ids_p = swap_line(ids)
    up0 = gather(up_f.reshape(cols, width))
    dy_p = swap_line(dy)
    up1 = swap_core(up0)
    down0 = gather(jnp.transpose(down_f, (0, 2, 1)).reshape(cols, hidden))
    x_p = swap_line(x)
    down1 = swap_core(down0)

    col = jnp.arange(layers * cols, dtype=jnp.int32)[None, :]
    label0 = ((col // cols) * plane + me % plane) * tenants + (col // rank) % tenants
    label1 = label0 + jnp.where(me % 2 == 0, tenants, -tenants)
    ids_of = (ids, ids_p)
    keep = [[i == lab for lab in (label0, label1)] for i in ids_of]
    xs, dys, ups, downs = (x, x_p), (dy, dy_p), (up0, up1), (down0, down1)

    def masked(v, k):
        return jnp.where(k, v, 0.0).astype(bf16)

    back = [[masked(dot_nt(dys[r], ups[c]), keep[r][c]) for c in range(2)] for r in range(2)]
    proj = [[masked(dot_nt(xs[r], downs[c]), keep[r][c]) for c in range(2)] for r in range(2)]

    def lora(coef, factors, r):
        return (
            adapter_scale * (dot_nn(coef[r][0], factors[0]) + dot_nn(coef[r][1], factors[1]))
        ).astype(bf16)

    def partial(coef, rows, c):
        return dot_tn(coef[0][c], rows[0]) + dot_tn(coef[1][c], rows[1])

    ga = scatter(
        (partial(back, xs, 0) + swap_core(partial(back, xs, 1).astype(bf16)).astype(f32)).astype(bf16)
    )
    gb = scatter(
        (partial(proj, dys, 0) + swap_core(partial(proj, dys, 1).astype(bf16)).astype(f32)).astype(bf16)
    )
    far_dx = swap_line(lora(back, downs, 1))
    far_y = swap_line(lora(proj, ups, 1))
    near_dx = lora(back, downs, 0)
    near_y = lora(proj, ups, 0)
    layer_out = (dot_nn(x, w) + (near_y.astype(f32) + far_y.astype(f32))).astype(bf16)
    grad_tokens = (dot_nt(dy, w) + (near_dx.astype(f32) + far_dx.astype(f32))).astype(bf16)

    ga = adapter_scale * ga.astype(f32)
    gb = adapter_scale * gb.astype(f32)
    norm = jnp.sqrt(lax.psum(jnp.sum(ga * ga) + jnp.sum(gb * gb), "dev"))
    entries = jnp.sqrt(f32(tenants * n * rank * (hidden + width)))
    factor = jnp.minimum(f32(1.0), entries / (norm + 1e-06))
    grad_a = jnp.transpose((ga * factor).astype(bf16).reshape(tenants, rank, hidden), (0, 2, 1))
    grad_b = (gb * factor).astype(bf16).reshape(tenants, rank, width)
    return (layer_out, grad_tokens, grad_a, grad_b)


def copy_to(src, dst, send_sem, recv_sem, device):
    return pltpu.make_async_remote_copy(
        src_ref=src,
        dst_ref=dst,
        send_sem=send_sem,
        recv_sem=recv_sem,
        device_id={"dev": device},
        device_id_type=pl.DeviceIdType.MESH,
    )


def greet(barrier, device):
    pl.semaphore_signal(
        barrier, inc=1, device_id={"dev": device}, device_id_type=pl.DeviceIdType.MESH
    )


def position():
    me = lax.axis_index("dev")
    z, core = me // plane, me % 2
    return me, z, core, me + 1 - 2 * core


def gather_kernel(
    layers,
    down,
    up,
    x,
    dy,
    w,
    down_all,
    up_all,
    frozen_y,
    frozen_dx,
    w_vmem,
    w_sem,
    own_sem,
    send,
    recv,
    core_send,
    core_recv,
):
    load = pltpu.make_async_copy(w, w_vmem, w_sem)
    load.start()
    me, z, core, twin = position()
    steps = layers - 1
    arrays = ((down, down_all), (up, up_all))
    inner = z > 0
    outer = z < layers - 1
    barrier = pltpu.get_barrier_semaphore()
    greet(barrier, twin)
    pl.when(inner)(lambda: greet(barrier, me - plane))
    pl.when(outer)(lambda: greet(barrier, me + plane))
    pl.semaphore_wait(barrier, 1 + inner.astype(jnp.int32) + outer.astype(jnp.int32))

    def hop(way, s, a):
        block = z - s if way == 0 else z + s
        own, whole = arrays[a]
        spot = whole.at[block, core]
        k = (way * steps + s) * 2 + a
        target = me + plane if way == 0 else me - plane
        return copy_to(own if s == 0 else spot, spot, send.at[k], recv.at[k], target)

    def landed(way, s, a):
        block = z - 1 - s if way == 0 else z + 1 + s
        own, whole = arrays[a]
        k = (way * steps + s) * 2 + a
        return copy_to(own, whole.at[block, core], send.at[k], recv.at[k], twin)

    def across(way, s, a):
        block = z - 1 - s if way == 0 else z + 1 + s
        spot = arrays[a][1].at[block, core]
        k = (way * steps + s) * 2 + a
        return copy_to(spot, spot, core_send.at[k], core_recv.at[k], twin)

    def from_twin(way, s, a):
        block = z - 1 - s if way == 0 else z + 1 + s
        spot = arrays[a][1].at[block, 1 - core]
        k = (way * steps + s) * 2 + a
        return copy_to(spot, spot, core_send.at[k], core_recv.at[k], twin)

    def sends(way, s):
        return (z >= s) & outer if way == 0 else (z + s <= layers - 1) & inner

    def arrives(way, s):
        return z - 1 - s >= 0 if way == 0 else z + 1 + s <= layers - 1

    def each(copies, act):
        def run():
            for a in range(2):
                act(copies(a))

        return run

    def start(c):
        c.start()

    base = 4 * steps

    def own_across(a):
        return copy_to(
            arrays[a][0],
            arrays[a][1].at[z, core],
            core_send.at[base + a],
            core_recv.at[base + a],
            twin,
        )

    def own_from(a):
        return copy_to(
            arrays[a][0],
            arrays[a][1].at[z, 1 - core],
            core_send.at[base + a],
            core_recv.at[base + a],
            twin,
        )

    def own_copy(a):
        return pltpu.make_async_copy(arrays[a][0], arrays[a][1].at[z, core], own_sem.at[a])

    for s in range(steps):
        for way in range(2):
            pl.when(sends(way, s))(each(functools.partial(hop, way, s), start))
        if s == 0:
            each(own_across, start)()
            each(own_copy, start)()
            load.wait()
            frozen_y[...] = jnp.zeros_like(frozen_y)

            def products(i, carry):
                part = pl.ds(pl.multiple_of(i * piece, piece), piece)
                block = w_vmem[part, :]
                frozen_y[...] += dot_nn(x[:, part], block)
                frozen_dx[:, part] = dot_nt(dy[...], block)
                return carry

            lax.fori_loop(0, w_vmem.shape[0] // piece, products, 0)
        for way in range(2):
            pl.when(arrives(way, s))(
                each(functools.partial(landed, way, s), lambda c: c.wait_recv())
            )
        for way in range(2):
            pl.when(arrives(way, s))(each(functools.partial(across, way, s), start))
    for a in range(2):
        own_copy(a).wait()
        own_across(a).wait_send()
        own_from(a).wait_recv()
    for s in range(steps):
        for way in range(2):
            pl.when(sends(way, s))(each(functools.partial(hop, way, s), lambda c: c.wait_send()))
            pl.when(arrives(way, s))(
                each(functools.partial(across, way, s), lambda c: c.wait_send())
            )
            pl.when(arrives(way, s))(
                each(functools.partial(from_twin, way, s), lambda c: c.wait_recv())
            )


def reduce_kernel(
    layers,
    rounds,
    limit,
    part_a,
    part_b,
    out_a,
    out_b,
    twin_a,
    twin_b,
    sum_a,
    sum_b,
    in_a,
    in_b,
    send_a,
    send_b,
    norm_buf,
    twin_send,
    twin_recv,
    hop_send,
    hop_recv,
    norm_send,
    norm_recv,
):
    me, z, core, twin = position()
    inner = z > 0
    outer = z < layers - 1
    arrays = (
        (part_a, twin_a, sum_a, in_a, send_a),
        (part_b, twin_b, sum_b, in_b, send_b),
    )
    partners = []
    for r in range(rounds):
        bit = 2**r
        partners.append(me + bit - 2 * bit * ((me // bit) % 2))
    barrier = pltpu.get_barrier_semaphore()
    for p in partners:
        greet(barrier, p)
    pl.when(inner)(lambda: greet(barrier, me - plane))
    pl.when(outer)(lambda: greet(barrier, me + plane))
    pl.semaphore_wait(barrier, rounds + inner.astype(jnp.int32) + outer.astype(jnp.int32))

    order = []
    for i in range((layers + 1) // 2):
        order += [layers - 1 - i, i] if layers - 1 - i != i else [i]

    def to_twin(j, a):
        part, got = arrays[a][:2]
        k = 2 * j + a
        return copy_to(part.at[j, 1 - core], got.at[j], twin_send.at[k], twin_recv.at[k], twin)

    for j in order:
        for a in range(2):
            to_twin(j, a).start()

    ready = set()

    def prepare(j):
        if j in ready:
            return
        ready.add(j)
        for a in range(2):
            part, got, total = arrays[a][:3]
            to_twin(j, a).wait_recv()
            total[j] = part[j, core].astype(f32) + got[j].astype(f32)

    def hop(way, j, a):
        k = (way * layers + j) * 2 + a
        return copy_to(
            arrays[a][4].at[way, j],
            arrays[a][3].at[way, j],
            hop_send.at[k],
            hop_recv.at[k],
            me + plane if way == 0 else me - plane,
        )

    def take(way, j):
        for a in range(2):
            total, came = arrays[a][2:4]
            hop(way, j, a).wait_recv()
            total[j] = total[j] + came[way, j].astype(f32)

    def forward(way, j):
        pl.when(inner if way == 0 else outer)(lambda: take(way, j))
        for a in range(2):
            total, _, out = arrays[a][2:]
            out[way, j] = total[j].astype(bf16)
            hop(way, j, a).start()

    lower = z < layers // 2

    def moves(way, j):
        return z < j if way == 0 else z > j

    for i in range(layers - 1):
        far, near = layers - 1 - i, i
        prepare(far)
        prepare(near)
        pl.when(moves(0, far) & lower)(functools.partial(forward, 0, far))
        pl.when(moves(1, near))(functools.partial(forward, 1, near))
        pl.when(moves(0, far) & ~lower)(functools.partial(forward, 0, far))
    for j in range(layers):
        prepare(j)
    for j in range(layers):
        if j > 0:
            pl.when(z == j)(functools.partial(take, 0, j))
        if j < layers - 1:
            pl.when(z == j)(functools.partial(take, 1, j))

    raw_a = sum_a[z] * adapter_scale
    raw_b = sum_b[z] * adapter_scale
    squares = jnp.sum(raw_a * raw_a) + jnp.sum(raw_b * raw_b)
    norm_buf[0] = jnp.full(norm_buf.shape[1:], squares, f32)
    for r, p in enumerate(partners):
        c = copy_to(norm_buf.at[2 * r], norm_buf.at[2 * r + 1], norm_send.at[r], norm_recv.at[r], p)
        c.start()
        c.wait()
        norm_buf[2 * r + 2] = norm_buf[2 * r] + norm_buf[2 * r + 1]
    norm = jnp.sqrt(norm_buf[2 * rounds][0:1, 0:1])
    factor = jnp.minimum(f32(1.0), f32(limit) / (norm + f32(1e-06)))
    out_a[...] = (sum_a[z] * adapter_scale * factor).astype(bf16)
    out_b[...] = (sum_b[z] * adapter_scale * factor).astype(bf16)

    for j in range(layers):
        for a in range(2):
            to_twin(j, a).wait_send()
        for way in range(2):
            if (way == 0 and j > 0) or (way == 1 and j < layers - 1):

                def settle(way=way, j=j):
                    for a in range(2):
                        hop(way, j, a).wait_send()

                pl.when(moves(way, j))(settle)


def gather_line(layers, down, up, x, dy, w):
    cols, hidden = down.shape
    width = up.shape[1]
    sems = 4 * (layers - 1)
    anywhere = pl.BlockSpec(memory_space=pl.ANY)
    vmem = pl.BlockSpec(memory_space=pltpu.VMEM)
    return pl.pallas_call(
        functools.partial(gather_kernel, layers),
        out_shape=(
            jax.ShapeDtypeStruct((layers, 2, cols, hidden), bf16),
            jax.ShapeDtypeStruct((layers, 2, cols, width), bf16),
            jax.ShapeDtypeStruct(dy.shape, f32),
            jax.ShapeDtypeStruct(x.shape, f32),
        ),
        in_specs=[anywhere, anywhere, vmem, vmem, anywhere],
        out_specs=[anywhere, anywhere, vmem, vmem],
        scratch_shapes=[
            pltpu.VMEM(w.shape, bf16),
            pltpu.SemaphoreType.DMA,
            pltpu.SemaphoreType.DMA((2,)),
            pltpu.SemaphoreType.DMA((sems,)),
            pltpu.SemaphoreType.DMA((sems,)),
            pltpu.SemaphoreType.DMA((sems + 2,)),
            pltpu.SemaphoreType.DMA((sems + 2,)),
        ],
        cost_estimate=pl.CostEstimate(flops=0, bytes_accessed=100_000_000, transcendentals=0),
        compiler_params=pltpu.CompilerParams(
            collective_id=0, has_side_effects=True, vmem_limit_bytes=40 * 2**20
        ),
    )(down, up, x, dy, w)


def reduce_line(layers, n, limit, part_a, part_b):
    _, _, cols, hidden = part_a.shape
    width = part_b.shape[3]
    rounds = n.bit_length() - 1
    vmem = pl.BlockSpec(memory_space=pltpu.VMEM)

    def both(lead, dtype):
        return [pltpu.VMEM((*lead, cols, m), dtype) for m in (hidden, width)]

    return pl.pallas_call(
        functools.partial(reduce_kernel, layers, rounds, limit),
        out_shape=(
            jax.ShapeDtypeStruct((cols, hidden), bf16),
            jax.ShapeDtypeStruct((cols, width), bf16),
        ),
        in_specs=[vmem] * 2,
        out_specs=[vmem] * 2,
        scratch_shapes=[
            *both((layers,), bf16),
            *both((layers,), f32),
            *both((2, layers), bf16),
            *both((2, layers), bf16),
            pltpu.VMEM((2 * rounds + 1, 8, 128), f32),
            pltpu.SemaphoreType.DMA((2 * layers,)),
            pltpu.SemaphoreType.DMA((2 * layers,)),
            pltpu.SemaphoreType.DMA((4 * layers,)),
            pltpu.SemaphoreType.DMA((4 * layers,)),
            pltpu.SemaphoreType.DMA((rounds,)),
            pltpu.SemaphoreType.DMA((rounds,)),
        ],
        cost_estimate=pl.CostEstimate(flops=0, bytes_accessed=100_000_000, transcendentals=0),
        compiler_params=pltpu.CompilerParams(
            collective_id=1, has_side_effects=True, vmem_limit_bytes=48 * 2**20
        ),
    )(part_a, part_b)


def short_line(x, dy, w, down_f, up_f, owner, slot):
    n = lax.axis_size("dev")
    me = lax.axis_index("dev")
    layers = n // plane
    tenants, hidden, rank = down_f.shape
    width = up_f.shape[2]
    cols = tenants * rank
    to_line = [(i, i ^ 2) for i in range(n)]

    def swap_line(v):
        return lax.ppermute(v, "dev", to_line)

    ids = (owner[:, 0] * tenants + slot).reshape(-1, 1)
    ids_p = swap_line(ids)
    dy_p = swap_line(dy)
    x_p = swap_line(x)
    downs, ups, frozen_y, frozen_dx = gather_line(
        layers,
        jnp.transpose(down_f, (0, 2, 1)).reshape(cols, hidden),
        up_f.reshape(cols, width),
        x,
        dy,
        w,
    )
    downs = downs.reshape(layers * 2 * cols, hidden)
    ups = ups.reshape(layers * 2 * cols, width)

    col = jnp.arange(layers * 2 * cols, dtype=jnp.int32)[None, :]
    device = (col // (2 * cols)) * plane + (me % plane) // 2 * 2 + (col // cols) % 2
    label = device * tenants + (col // rank) % tenants

    def masked(v, i):
        return jnp.where(i == label, v, 0.0).astype(bf16)

    back_p = masked(dot_nt(dy_p, ups), ids_p)
    far_dx = swap_line((adapter_scale * dot_nn(back_p, downs)).astype(bf16))
    proj_p = masked(dot_nt(x_p, downs), ids_p)
    far_y = swap_line((adapter_scale * dot_nn(proj_p, ups)).astype(bf16))
    back = masked(dot_nt(dy, ups), ids)
    proj = masked(dot_nt(x, downs), ids)
    part_a = (dot_tn(back, x) + dot_tn(back_p, x_p)).astype(bf16)
    part_b = (dot_tn(proj, dy) + dot_tn(proj_p, dy_p)).astype(bf16)
    near_dx = (adapter_scale * dot_nn(back, downs)).astype(bf16)
    near_y = (adapter_scale * dot_nn(proj, ups)).astype(bf16)
    limit = float(tenants * n * rank * (hidden + width)) ** 0.5
    grad_a, grad_b = reduce_line(
        layers,
        n,
        limit,
        part_a.reshape(layers, 2, cols, hidden),
        part_b.reshape(layers, 2, cols, width),
    )
    layer_out = (frozen_y + (near_y.astype(f32) + far_y.astype(f32))).astype(bf16)
    grad_tokens = (frozen_dx + (near_dx.astype(f32) + far_dx.astype(f32))).astype(bf16)
    grad_a = jnp.transpose(grad_a.reshape(tenants, rank, hidden), (0, 2, 1))
    return (layer_out, grad_tokens, grad_a, grad_b.reshape(tenants, rank, width))


def local(*args):
    if lax.axis_size("dev") // plane <= 4:
        return short_line(*args)
    return long_line(*args)


def solution(mesh):
    rows = P(("groups", "dev"), None)
    stack = P(("groups", "dev"), None, None)
    return jax.shard_map(
        local,
        mesh=mesh,
        in_specs=(rows, rows, P(), stack, stack, rows, P(("groups", "dev"))),
        out_specs=(rows, rows, stack, stack),
        check_vma=False,
    )
```

```python
import functools

import jax
import jax.numpy as jnp
from jax import lax
from jax.experimental import pallas as pl
from jax.experimental.pallas import tpu as pltpu
from jax.sharding import PartitionSpec as P

adapter_scale = 2.0
piece = 512
plane = 4
f32 = jnp.float32
bf16 = jnp.bfloat16


def dot_nn(a, b):
    return lax.dot_general(a, b, (((1,), (0,)), ((), ())), preferred_element_type=f32)


def dot_nt(a, b):
    return lax.dot_general(a, b, (((1,), (1,)), ((), ())), preferred_element_type=f32)


def dot_tn(a, b):
    return lax.dot_general(a, b, (((0,), (0,)), ((), ())), preferred_element_type=f32)


def long_line(x, dy, w, down_f, up_f, owner, slot):
    n = lax.axis_size("dev")
    me = lax.axis_index("dev")
    layers = n // plane
    tenants, hidden, rank = down_f.shape
    width = up_f.shape[2]
    cols = tenants * rank
    columns = [[z * plane + k for z in range(layers)] for k in range(plane)]
    to_core = [(i, i ^ 1) for i in range(n)]
    to_line = [(i, i ^ 2) for i in range(n)]

    def gather(v):
        return lax.all_gather(v, "dev", axis_index_groups=columns, tiled=True)

    def scatter(v):
        return lax.psum_scatter(
            v, "dev", scatter_dimension=0, axis_index_groups=columns, tiled=True
        )

    def swap_core(v):
        return lax.ppermute(v, "dev", to_core)

    def swap_line(v):
        return lax.ppermute(v, "dev", to_line)

    ids = (owner[:, 0] * tenants + slot).reshape(-1, 1)
    ids_p = swap_line(ids)
    up0 = gather(up_f.reshape(cols, width))
    dy_p = swap_line(dy)
    up1 = swap_core(up0)
    down0 = gather(jnp.transpose(down_f, (0, 2, 1)).reshape(cols, hidden))
    x_p = swap_line(x)
    down1 = swap_core(down0)

    col = jnp.arange(layers * cols, dtype=jnp.int32)[None, :]
    label0 = ((col // cols) * plane + me % plane) * tenants + (col // rank) % tenants
    label1 = label0 + jnp.where(me % 2 == 0, tenants, -tenants)
    ids_of = (ids, ids_p)
    keep = [[i == lab for lab in (label0, label1)] for i in ids_of]
    xs, dys, ups, downs = (x, x_p), (dy, dy_p), (up0, up1), (down0, down1)

    def masked(v, k):
        return jnp.where(k, v, 0.0).astype(bf16)

    back = [[masked(dot_nt(dys[r], ups[c]), keep[r][c]) for c in range(2)] for r in range(2)]
    proj = [[masked(dot_nt(xs[r], downs[c]), keep[r][c]) for c in range(2)] for r in range(2)]

    def lora(coef, factors, r):
        return (
            adapter_scale * (dot_nn(coef[r][0], factors[0]) + dot_nn(coef[r][1], factors[1]))
        ).astype(bf16)

    def partial(coef, rows, c):
        return dot_tn(coef[0][c], rows[0]) + dot_tn(coef[1][c], rows[1])

    ga = scatter(
        (partial(back, xs, 0) + swap_core(partial(back, xs, 1).astype(bf16)).astype(f32)).astype(bf16)
    )
    gb = scatter(
        (partial(proj, dys, 0) + swap_core(partial(proj, dys, 1).astype(bf16)).astype(f32)).astype(bf16)
    )
    far_dx = swap_line(lora(back, downs, 1))
    far_y = swap_line(lora(proj, ups, 1))
    near_dx = lora(back, downs, 0)
    near_y = lora(proj, ups, 0)
    layer_out = (dot_nn(x, w) + (near_y.astype(f32) + far_y.astype(f32))).astype(bf16)
    grad_tokens = (dot_nt(dy, w) + (near_dx.astype(f32) + far_dx.astype(f32))).astype(bf16)

    ga = adapter_scale * ga.astype(f32)
    gb = adapter_scale * gb.astype(f32)
    norm = jnp.sqrt(lax.psum(jnp.sum(ga * ga) + jnp.sum(gb * gb), "dev"))
    entries = jnp.sqrt(f32(tenants * n * rank * (hidden + width)))
    factor = jnp.minimum(f32(1.0), entries / (norm + 1e-06))
    grad_a = jnp.transpose((ga * factor).astype(bf16).reshape(tenants, rank, hidden), (0, 2, 1))
    grad_b = (gb * factor).astype(bf16).reshape(tenants, rank, width)
    return (layer_out, grad_tokens, grad_a, grad_b)


def copy_to(src, dst, send_sem, recv_sem, device):
    return pltpu.make_async_remote_copy(
        src_ref=src,
        dst_ref=dst,
        send_sem=send_sem,
        recv_sem=recv_sem,
        device_id={"dev": device},
        device_id_type=pl.DeviceIdType.MESH,
    )


def greet(barrier, device):
    pl.semaphore_signal(
        barrier, inc=1, device_id={"dev": device}, device_id_type=pl.DeviceIdType.MESH
    )


def position():
    me = lax.axis_index("dev")
    z, core = me // plane, me % 2
    return me, z, core, me + 1 - 2 * core


def gather_kernel(
    layers,
    down,
    up,
    x,
    dy,
    w,
    down_all,
    up_all,
    frozen_y,
    frozen_dx,
    x_line,
    dy_line,
    w_vmem,
    w_sem,
    line_send,
    line_recv,
    own_sem,
    send,
    recv,
    core_send,
    core_recv,
):
    load = pltpu.make_async_copy(w, w_vmem, w_sem)
    load.start()
    me, z, core, twin = position()
    across_y = me + 2 - 4 * ((me // 2) % 2)
    steps = layers - 1
    arrays = ((down, down_all), (up, up_all))
    inner = z > 0
    outer = z < layers - 1
    barrier = pltpu.get_barrier_semaphore()
    greet(barrier, twin)
    greet(barrier, across_y)
    pl.when(inner)(lambda: greet(barrier, me - plane))
    pl.when(outer)(lambda: greet(barrier, me + plane))
    pl.semaphore_wait(barrier, 2 + inner.astype(jnp.int32) + outer.astype(jnp.int32))
    rows = [
        copy_to(dy, dy_line, line_send.at[0], line_recv.at[0], across_y),
        copy_to(x, x_line, line_send.at[1], line_recv.at[1], across_y),
    ]

    def hop(way, s, a):
        block = z - s if way == 0 else z + s
        own, whole = arrays[a]
        spot = whole.at[block, core]
        k = (way * steps + s) * 2 + a
        target = me + plane if way == 0 else me - plane
        return copy_to(own if s == 0 else spot, spot, send.at[k], recv.at[k], target)

    def landed(way, s, a):
        block = z - 1 - s if way == 0 else z + 1 + s
        own, whole = arrays[a]
        k = (way * steps + s) * 2 + a
        return copy_to(own, whole.at[block, core], send.at[k], recv.at[k], twin)

    def across(way, s, a):
        block = z - 1 - s if way == 0 else z + 1 + s
        spot = arrays[a][1].at[block, core]
        k = (way * steps + s) * 2 + a
        return copy_to(spot, spot, core_send.at[k], core_recv.at[k], twin)

    def from_twin(way, s, a):
        block = z - 1 - s if way == 0 else z + 1 + s
        spot = arrays[a][1].at[block, 1 - core]
        k = (way * steps + s) * 2 + a
        return copy_to(spot, spot, core_send.at[k], core_recv.at[k], twin)

    def sends(way, s):
        return (z >= s) & outer if way == 0 else (z + s <= layers - 1) & inner

    def arrives(way, s):
        return z - 1 - s >= 0 if way == 0 else z + 1 + s <= layers - 1

    def each(copies, act):
        def run():
            for a in range(2):
                act(copies(a))

        return run

    def start(c):
        c.start()

    base = 4 * steps

    def own_across(a):
        return copy_to(
            arrays[a][0],
            arrays[a][1].at[z, core],
            core_send.at[base + a],
            core_recv.at[base + a],
            twin,
        )

    def own_from(a):
        return copy_to(
            arrays[a][0],
            arrays[a][1].at[z, 1 - core],
            core_send.at[base + a],
            core_recv.at[base + a],
            twin,
        )

    def own_copy(a):
        return pltpu.make_async_copy(arrays[a][0], arrays[a][1].at[z, core], own_sem.at[a])

    for s in range(steps):
        for way in range(2):
            pl.when(sends(way, s))(each(functools.partial(hop, way, s), start))
        if s == 0:
            for c in rows:
                c.start()
            each(own_across, start)()
            each(own_copy, start)()
            load.wait()
            frozen_y[...] = jnp.zeros_like(frozen_y)

            def products(i, carry):
                part = pl.ds(pl.multiple_of(i * piece, piece), piece)
                block = w_vmem[part, :]
                frozen_y[...] += dot_nn(x[:, part], block)
                frozen_dx[:, part] = dot_nt(dy[...], block)
                return carry

            lax.fori_loop(0, w_vmem.shape[0] // piece, products, 0)
        for way in range(2):
            pl.when(arrives(way, s))(
                each(functools.partial(landed, way, s), lambda c: c.wait_recv())
            )
        for way in range(2):
            pl.when(arrives(way, s))(each(functools.partial(across, way, s), start))
    for c in rows:
        c.wait()
    for a in range(2):
        own_copy(a).wait()
        own_across(a).wait_send()
        own_from(a).wait_recv()
    for s in range(steps):
        for way in range(2):
            pl.when(sends(way, s))(each(functools.partial(hop, way, s), lambda c: c.wait_send()))
            pl.when(arrives(way, s))(
                each(functools.partial(across, way, s), lambda c: c.wait_send())
            )
            pl.when(arrives(way, s))(
                each(functools.partial(from_twin, way, s), lambda c: c.wait_recv())
            )


def reduce_kernel(
    layers,
    limit,
    part_a,
    part_b,
    out_a,
    out_b,
    twin_a,
    twin_b,
    sum_a,
    sum_b,
    in_a,
    in_b,
    send_a,
    send_b,
    norm_buf,
    twin_send,
    twin_recv,
    hop_send,
    hop_recv,
    norm_send,
    norm_recv,
):
    me, z, core, twin = position()
    inner = z > 0
    outer = z < layers - 1
    arrays = (
        (part_a, twin_a, sum_a, in_a, send_a),
        (part_b, twin_b, sum_b, in_b, send_b),
    )
    def in_plane(k):
        return me - me % plane + (me % plane + k) % plane

    def in_column(k):
        return (z + k) % layers * plane + me % plane

    barrier = pltpu.get_barrier_semaphore()
    for k in range(1, plane):
        greet(barrier, in_plane(k))
    for k in range(1, layers):
        greet(barrier, in_column(k))
    pl.semaphore_wait(barrier, plane + layers - 2)

    order = []
    for i in range((layers + 1) // 2):
        order += [layers - 1 - i, i] if layers - 1 - i != i else [i]

    def to_twin(j, a):
        part, got = arrays[a][:2]
        k = 2 * j + a
        return copy_to(part.at[j, 1 - core], got.at[j], twin_send.at[k], twin_recv.at[k], twin)

    for j in order:
        for a in range(2):
            to_twin(j, a).start()

    ready = set()

    def prepare(j):
        if j in ready:
            return
        ready.add(j)
        for a in range(2):
            part, got, total = arrays[a][:3]
            to_twin(j, a).wait_recv()
            total[j] = part[j, core].astype(f32) + got[j].astype(f32)

    def hop(way, j, a):
        k = (way * layers + j) * 2 + a
        return copy_to(
            arrays[a][4].at[way, j],
            arrays[a][3].at[way, j],
            hop_send.at[k],
            hop_recv.at[k],
            me + plane if way == 0 else me - plane,
        )

    def take(way, j):
        for a in range(2):
            total, came = arrays[a][2:4]
            hop(way, j, a).wait_recv()
            total[j] = total[j] + came[way, j].astype(f32)

    def forward(way, j):
        pl.when(inner if way == 0 else outer)(lambda: take(way, j))
        for a in range(2):
            total, _, out = arrays[a][2:]
            out[way, j] = total[j].astype(bf16)
            hop(way, j, a).start()

    lower = z < layers // 2

    def moves(way, j):
        return z < j if way == 0 else z > j

    for i in range(layers - 1):
        far, near = layers - 1 - i, i
        prepare(far)
        prepare(near)
        pl.when(moves(0, far) & lower)(functools.partial(forward, 0, far))
        pl.when(moves(1, near))(functools.partial(forward, 1, near))
        pl.when(moves(0, far) & ~lower)(functools.partial(forward, 0, far))
    for j in range(layers):
        prepare(j)
    for j in range(layers):
        if j > 0:
            pl.when(z == j)(functools.partial(take, 0, j))
        if j < layers - 1:
            pl.when(z == j)(functools.partial(take, 1, j))

    raw_a = sum_a[z] * adapter_scale
    raw_b = sum_b[z] * adapter_scale
    squares = jnp.sum(raw_a * raw_a) + jnp.sum(raw_b * raw_b)
    norm_buf[0] = jnp.full(norm_buf.shape[1:], squares, f32)

    def share(first, count, target):
        copies = []
        for k in range(1, count):
            at = first + k
            copies.append(
                copy_to(
                    norm_buf.at[first], norm_buf.at[at], norm_send.at[at], norm_recv.at[at], target(k)
                )
            )
            copies[-1].start()
        total = norm_buf[first]
        for k, c in enumerate(copies):
            c.wait()
            total = total + norm_buf[first + 1 + k]
        return total

    norm_buf[plane] = share(0, plane, in_plane)
    norm = jnp.sqrt(share(plane, layers, in_column)[0:1, 0:1])
    factor = jnp.minimum(f32(1.0), f32(limit) / (norm + f32(1e-06)))
    out_a[...] = (sum_a[z] * adapter_scale * factor).astype(bf16)
    out_b[...] = (sum_b[z] * adapter_scale * factor).astype(bf16)

    for j in range(layers):
        for a in range(2):
            to_twin(j, a).wait_send()
        for way in range(2):
            if (way == 0 and j > 0) or (way == 1 and j < layers - 1):

                def settle(way=way, j=j):
                    for a in range(2):
                        hop(way, j, a).wait_send()

                pl.when(moves(way, j))(settle)


def gather_line(layers, down, up, x, dy, w):
    cols, hidden = down.shape
    width = up.shape[1]
    sems = 4 * (layers - 1)
    anywhere = pl.BlockSpec(memory_space=pl.ANY)
    vmem = pl.BlockSpec(memory_space=pltpu.VMEM)
    return pl.pallas_call(
        functools.partial(gather_kernel, layers),
        out_shape=(
            jax.ShapeDtypeStruct((layers, 2, cols, hidden), bf16),
            jax.ShapeDtypeStruct((layers, 2, cols, width), bf16),
            jax.ShapeDtypeStruct(dy.shape, f32),
            jax.ShapeDtypeStruct(x.shape, f32),
            jax.ShapeDtypeStruct(x.shape, bf16),
            jax.ShapeDtypeStruct(dy.shape, bf16),
        ),
        in_specs=[anywhere, anywhere, vmem, vmem, anywhere],
        out_specs=[anywhere, anywhere, vmem, vmem, anywhere, anywhere],
        scratch_shapes=[
            pltpu.VMEM(w.shape, bf16),
            pltpu.SemaphoreType.DMA,
            pltpu.SemaphoreType.DMA((2,)),
            pltpu.SemaphoreType.DMA((2,)),
            pltpu.SemaphoreType.DMA((2,)),
            pltpu.SemaphoreType.DMA((sems,)),
            pltpu.SemaphoreType.DMA((sems,)),
            pltpu.SemaphoreType.DMA((sems + 2,)),
            pltpu.SemaphoreType.DMA((sems + 2,)),
        ],
        cost_estimate=pl.CostEstimate(flops=0, bytes_accessed=100_000_000, transcendentals=0),
        compiler_params=pltpu.CompilerParams(
            collective_id=0, has_side_effects=True, vmem_limit_bytes=40 * 2**20
        ),
    )(down, up, x, dy, w)


def reduce_line(layers, limit, part_a, part_b):
    _, _, cols, hidden = part_a.shape
    width = part_b.shape[3]
    vmem = pl.BlockSpec(memory_space=pltpu.VMEM)

    def both(lead, dtype):
        return [pltpu.VMEM((*lead, cols, m), dtype) for m in (hidden, width)]

    return pl.pallas_call(
        functools.partial(reduce_kernel, layers, limit),
        out_shape=(
            jax.ShapeDtypeStruct((cols, hidden), bf16),
            jax.ShapeDtypeStruct((cols, width), bf16),
        ),
        in_specs=[vmem] * 2,
        out_specs=[vmem] * 2,
        scratch_shapes=[
            *both((layers,), bf16),
            *both((layers,), f32),
            *both((2, layers), bf16),
            *both((2, layers), bf16),
            pltpu.VMEM((plane + layers, 8, 128), f32),
            pltpu.SemaphoreType.DMA((2 * layers,)),
            pltpu.SemaphoreType.DMA((2 * layers,)),
            pltpu.SemaphoreType.DMA((4 * layers,)),
            pltpu.SemaphoreType.DMA((4 * layers,)),
            pltpu.SemaphoreType.DMA((plane + layers,)),
            pltpu.SemaphoreType.DMA((plane + layers,)),
        ],
        cost_estimate=pl.CostEstimate(flops=0, bytes_accessed=100_000_000, transcendentals=0),
        compiler_params=pltpu.CompilerParams(
            collective_id=1, has_side_effects=True, vmem_limit_bytes=48 * 2**20
        ),
    )(part_a, part_b)


def short_line(x, dy, w, down_f, up_f, owner, slot):
    n = lax.axis_size("dev")
    me = lax.axis_index("dev")
    layers = n // plane
    tenants, hidden, rank = down_f.shape
    width = up_f.shape[2]
    cols = tenants * rank
    to_line = [(i, i ^ 2) for i in range(n)]

    def swap_line(v):
        return lax.ppermute(v, "dev", to_line)

    ids = (owner[:, 0] * tenants + slot).reshape(-1, 1)
    ids_p = swap_line(ids)
    downs, ups, frozen_y, frozen_dx, x_p, dy_p = gather_line(
        layers,
        jnp.transpose(down_f, (0, 2, 1)).reshape(cols, hidden),
        up_f.reshape(cols, width),
        x,
        dy,
        w,
    )
    downs = downs.reshape(layers * 2 * cols, hidden)
    ups = ups.reshape(layers * 2 * cols, width)

    col = jnp.arange(layers * 2 * cols, dtype=jnp.int32)[None, :]
    device = (col // (2 * cols)) * plane + (me % plane) // 2 * 2 + (col // cols) % 2
    label = device * tenants + (col // rank) % tenants

    def masked(v, i):
        return jnp.where(i == label, v, 0.0).astype(bf16)

    back_p = masked(dot_nt(dy_p, ups), ids_p)
    far_dx = swap_line((adapter_scale * dot_nn(back_p, downs)).astype(bf16))
    proj_p = masked(dot_nt(x_p, downs), ids_p)
    far_y = swap_line((adapter_scale * dot_nn(proj_p, ups)).astype(bf16))
    back = masked(dot_nt(dy, ups), ids)
    proj = masked(dot_nt(x, downs), ids)
    part_a = (dot_tn(back, x) + dot_tn(back_p, x_p)).astype(bf16)
    part_b = (dot_tn(proj, dy) + dot_tn(proj_p, dy_p)).astype(bf16)
    near_dx = (adapter_scale * dot_nn(back, downs)).astype(bf16)
    near_y = (adapter_scale * dot_nn(proj, ups)).astype(bf16)
    limit = float(tenants * n * rank * (hidden + width)) ** 0.5
    grad_a, grad_b = reduce_line(
        layers,
        limit,
        part_a.reshape(layers, 2, cols, hidden),
        part_b.reshape(layers, 2, cols, width),
    )
    layer_out = (frozen_y + (near_y.astype(f32) + far_y.astype(f32))).astype(bf16)
    grad_tokens = (frozen_dx + (near_dx.astype(f32) + far_dx.astype(f32))).astype(bf16)
    grad_a = jnp.transpose(grad_a.reshape(tenants, rank, hidden), (0, 2, 1))
    return (layer_out, grad_tokens, grad_a, grad_b.reshape(tenants, rank, width))


def local(*args):
    if lax.axis_size("dev") // plane <= 4:
        return short_line(*args)
    return long_line(*args)


def solution(mesh):
    rows = P(("groups", "dev"), None)
    stack = P(("groups", "dev"), None, None)
    return jax.shard_map(
        local,
        mesh=mesh,
        in_specs=(rows, rows, P(), stack, stack, rows, P(("groups", "dev"))),
        out_specs=(rows, rows, stack, stack),
        check_vma=False,
    )
```

```python
import functools

import jax
import jax.numpy as jnp
from jax import lax
from jax.experimental import pallas as pl
from jax.experimental.pallas import tpu as pltpu
from jax.sharding import PartitionSpec as P

adapter_scale = 2.0
piece = 512
plane = 4
f32 = jnp.float32
bf16 = jnp.bfloat16


def dot_nn(a, b):
    return lax.dot_general(a, b, (((1,), (0,)), ((), ())), preferred_element_type=f32)


def dot_nt(a, b):
    return lax.dot_general(a, b, (((1,), (1,)), ((), ())), preferred_element_type=f32)


def dot_tn(a, b):
    return lax.dot_general(a, b, (((0,), (0,)), ((), ())), preferred_element_type=f32)


def long_line(x, dy, w, down_f, up_f, owner, slot):
    n = lax.axis_size("dev")
    me = lax.axis_index("dev")
    layers = n // plane
    tenants, hidden, rank = down_f.shape
    width = up_f.shape[2]
    cols = tenants * rank
    columns = [[z * plane + k for z in range(layers)] for k in range(plane)]
    to_core = [(i, i ^ 1) for i in range(n)]
    to_line = [(i, i ^ 2) for i in range(n)]

    def gather(v):
        return lax.all_gather(v, "dev", axis_index_groups=columns, tiled=True)

    def scatter(v):
        return lax.psum_scatter(
            v, "dev", scatter_dimension=0, axis_index_groups=columns, tiled=True
        )

    def swap_core(v):
        return lax.ppermute(v, "dev", to_core)

    def swap_line(v):
        return lax.ppermute(v, "dev", to_line)

    ids = (owner[:, 0] * tenants + slot).reshape(-1, 1)
    ids_p = swap_line(ids)
    up0 = gather(up_f.reshape(cols, width))
    dy_p = swap_line(dy)
    up1 = swap_core(up0)
    down0 = gather(jnp.transpose(down_f, (0, 2, 1)).reshape(cols, hidden))
    x_p = swap_line(x)
    down1 = swap_core(down0)

    col = jnp.arange(layers * cols, dtype=jnp.int32)[None, :]
    label0 = ((col // cols) * plane + me % plane) * tenants + (col // rank) % tenants
    label1 = label0 + jnp.where(me % 2 == 0, tenants, -tenants)
    ids_of = (ids, ids_p)
    keep = [[i == lab for lab in (label0, label1)] for i in ids_of]
    xs, dys, ups, downs = (x, x_p), (dy, dy_p), (up0, up1), (down0, down1)

    def masked(v, k):
        return jnp.where(k, v, 0.0).astype(bf16)

    back = [[masked(dot_nt(dys[r], ups[c]), keep[r][c]) for c in range(2)] for r in range(2)]
    proj = [[masked(dot_nt(xs[r], downs[c]), keep[r][c]) for c in range(2)] for r in range(2)]

    def lora(coef, factors, r):
        return (
            adapter_scale * (dot_nn(coef[r][0], factors[0]) + dot_nn(coef[r][1], factors[1]))
        ).astype(bf16)

    def partial(coef, rows, c):
        return dot_tn(coef[0][c], rows[0]) + dot_tn(coef[1][c], rows[1])

    ga = scatter(
        (partial(back, xs, 0) + swap_core(partial(back, xs, 1).astype(bf16)).astype(f32)).astype(bf16)
    )
    gb = scatter(
        (partial(proj, dys, 0) + swap_core(partial(proj, dys, 1).astype(bf16)).astype(f32)).astype(bf16)
    )
    far_dx = swap_line(lora(back, downs, 1))
    far_y = swap_line(lora(proj, ups, 1))
    near_dx = lora(back, downs, 0)
    near_y = lora(proj, ups, 0)
    layer_out = (dot_nn(x, w) + (near_y.astype(f32) + far_y.astype(f32))).astype(bf16)
    grad_tokens = (dot_nt(dy, w) + (near_dx.astype(f32) + far_dx.astype(f32))).astype(bf16)

    ga = adapter_scale * ga.astype(f32)
    gb = adapter_scale * gb.astype(f32)
    norm = jnp.sqrt(lax.psum(jnp.sum(ga * ga) + jnp.sum(gb * gb), "dev"))
    entries = jnp.sqrt(f32(tenants * n * rank * (hidden + width)))
    factor = jnp.minimum(f32(1.0), entries / (norm + 1e-06))
    grad_a = jnp.transpose((ga * factor).astype(bf16).reshape(tenants, rank, hidden), (0, 2, 1))
    grad_b = (gb * factor).astype(bf16).reshape(tenants, rank, width)
    return (layer_out, grad_tokens, grad_a, grad_b)


def copy_to(src, dst, send_sem, recv_sem, device):
    return pltpu.make_async_remote_copy(
        src_ref=src,
        dst_ref=dst,
        send_sem=send_sem,
        recv_sem=recv_sem,
        device_id={"dev": device},
        device_id_type=pl.DeviceIdType.MESH,
    )


def greet(barrier, device):
    pl.semaphore_signal(
        barrier, inc=1, device_id={"dev": device}, device_id_type=pl.DeviceIdType.MESH
    )


def position():
    me = lax.axis_index("dev")
    z, core = me // plane, me % 2
    return me, z, core, me + 1 - 2 * core


def gather_kernel(
    layers,
    down,
    up,
    x,
    dy,
    w,
    down_all,
    up_all,
    frozen_y,
    frozen_dx,
    x_line,
    dy_line,
    w_vmem,
    w_sem,
    line_send,
    line_recv,
    own_sem,
    send,
    recv,
    core_send,
    core_recv,
):
    load = pltpu.make_async_copy(w, w_vmem, w_sem)
    load.start()
    me, z, core, twin = position()
    across_y = me + 2 - 4 * ((me // 2) % 2)
    steps = layers - 1
    arrays = ((down, down_all), (up, up_all))
    inner = z > 0
    outer = z < layers - 1
    barrier = pltpu.get_barrier_semaphore()
    greet(barrier, twin)
    greet(barrier, across_y)
    pl.when(inner)(lambda: greet(barrier, me - plane))
    pl.when(outer)(lambda: greet(barrier, me + plane))
    pl.semaphore_wait(barrier, 2 + inner.astype(jnp.int32) + outer.astype(jnp.int32))
    rows = [
        copy_to(dy, dy_line, line_send.at[0], line_recv.at[0], across_y),
        copy_to(x, x_line, line_send.at[1], line_recv.at[1], across_y),
    ]

    def hop(way, s, a):
        block = z - s if way == 0 else z + s
        own, whole = arrays[a]
        spot = whole.at[block, core]
        k = (way * steps + s) * 2 + a
        target = me + plane if way == 0 else me - plane
        return copy_to(own if s == 0 else spot, spot, send.at[k], recv.at[k], target)

    def landed(way, s, a):
        block = z - 1 - s if way == 0 else z + 1 + s
        own, whole = arrays[a]
        k = (way * steps + s) * 2 + a
        return copy_to(own, whole.at[block, core], send.at[k], recv.at[k], twin)

    def across(way, s, a):
        block = z - 1 - s if way == 0 else z + 1 + s
        spot = arrays[a][1].at[block, core]
        k = (way * steps + s) * 2 + a
        return copy_to(spot, spot, core_send.at[k], core_recv.at[k], twin)

    def from_twin(way, s, a):
        block = z - 1 - s if way == 0 else z + 1 + s
        spot = arrays[a][1].at[block, 1 - core]
        k = (way * steps + s) * 2 + a
        return copy_to(spot, spot, core_send.at[k], core_recv.at[k], twin)

    def sends(way, s):
        return (z >= s) & outer if way == 0 else (z + s <= layers - 1) & inner

    def arrives(way, s):
        return z - 1 - s >= 0 if way == 0 else z + 1 + s <= layers - 1

    def each(copies, act):
        def run():
            for a in range(2):
                act(copies(a))

        return run

    def start(c):
        c.start()

    base = 4 * steps

    def own_across(a):
        return copy_to(
            arrays[a][0],
            arrays[a][1].at[z, core],
            core_send.at[base + a],
            core_recv.at[base + a],
            twin,
        )

    def own_from(a):
        return copy_to(
            arrays[a][0],
            arrays[a][1].at[z, 1 - core],
            core_send.at[base + a],
            core_recv.at[base + a],
            twin,
        )

    def own_copy(a):
        return pltpu.make_async_copy(arrays[a][0], arrays[a][1].at[z, core], own_sem.at[a])

    for s in range(steps):
        for way in range(2):
            pl.when(sends(way, s))(each(functools.partial(hop, way, s), start))
        if s == 0:
            for c in rows:
                c.start()
            each(own_across, start)()
            each(own_copy, start)()
            load.wait()
            frozen_y[...] = jnp.zeros_like(frozen_y)

            def products(i, carry):
                part = pl.ds(pl.multiple_of(i * piece, piece), piece)
                block = w_vmem[part, :]
                frozen_y[...] += dot_nn(x[:, part], block)
                frozen_dx[:, part] = dot_nt(dy[...], block)
                return carry

            lax.fori_loop(0, w_vmem.shape[0] // piece, products, 0)
        for way in range(2):
            pl.when(arrives(way, s))(
                each(functools.partial(landed, way, s), lambda c: c.wait_recv())
            )
        for way in range(2):
            pl.when(arrives(way, s))(each(functools.partial(across, way, s), start))
    for c in rows:
        c.wait()
    for a in range(2):
        own_copy(a).wait()
        own_across(a).wait_send()
        own_from(a).wait_recv()
    for s in range(steps):
        for way in range(2):
            pl.when(sends(way, s))(each(functools.partial(hop, way, s), lambda c: c.wait_send()))
            pl.when(arrives(way, s))(
                each(functools.partial(across, way, s), lambda c: c.wait_send())
            )
            pl.when(arrives(way, s))(
                each(functools.partial(from_twin, way, s), lambda c: c.wait_recv())
            )


def reduce_kernel(
    layers,
    limit,
    part_a,
    part_b,
    out_a,
    out_b,
    twin_a,
    twin_b,
    sum_a,
    sum_b,
    in_a,
    in_b,
    send_a,
    send_b,
    norm_buf,
    twin_send,
    twin_recv,
    hop_send,
    hop_recv,
    norm_send,
    norm_recv,
):
    me, z, core, twin = position()
    inner = z > 0
    outer = z < layers - 1
    arrays = (
        (part_a, twin_a, sum_a, in_a, send_a),
        (part_b, twin_b, sum_b, in_b, send_b),
    )
    def in_plane(k):
        return me - me % plane + (me % plane + k) % plane

    def in_column(k):
        return (z + k) % layers * plane + me % plane

    barrier = pltpu.get_barrier_semaphore()
    for k in range(1, plane):
        greet(barrier, in_plane(k))
    for k in range(1, layers):
        greet(barrier, in_column(k))
    pl.semaphore_wait(barrier, plane + layers - 2)

    lower = z < layers // 2
    order = []
    for i in range(layers // 2):
        order += [jnp.where(lower, layers - 1 - i, i), jnp.where(lower, i, layers - 1 - i)]
    if layers % 2:
        order.append(layers // 2)

    def to_twin(j, a):
        part, got = arrays[a][:2]
        k = 2 * j + a
        return copy_to(part.at[j, 1 - core], got.at[j], twin_send.at[k], twin_recv.at[k], twin)

    for j in order:
        for a in range(2):
            to_twin(j, a).start()

    def prepare(j):
        for a in range(2):
            part, got, total = arrays[a][:3]
            to_twin(j, a).wait_recv()
            total[j] = part[j, core].astype(f32) + got[j].astype(f32)

    def hop(way, j, a):
        k = (way * layers + j) * 2 + a
        return copy_to(
            arrays[a][4].at[way, j],
            arrays[a][3].at[way, j],
            hop_send.at[k],
            hop_recv.at[k],
            me + plane if way == 0 else me - plane,
        )

    def take(way, j):
        for a in range(2):
            total, came = arrays[a][2:4]
            hop(way, j, a).wait_recv()
            total[j] = total[j] + came[way, j].astype(f32)

    def forward(way, j):
        pl.when(inner if way == 0 else outer)(lambda: take(way, j))
        for a in range(2):
            total, _, out = arrays[a][2:]
            out[way, j] = total[j].astype(bf16)
            hop(way, j, a).start()

    def moves(way, j):
        return z < j if way == 0 else z > j

    for i in range(layers - 1):
        far, near = layers - 1 - i, i
        if 2 * i < layers:
            prepare(order[2 * i])
        pl.when(moves(0, far) & lower)(functools.partial(forward, 0, far))
        pl.when(moves(1, near) & ~lower)(functools.partial(forward, 1, near))
        if 2 * i + 1 < layers:
            prepare(order[2 * i + 1])
        pl.when(moves(1, near) & lower)(functools.partial(forward, 1, near))
        pl.when(moves(0, far) & ~lower)(functools.partial(forward, 0, far))
    for j in range(layers):
        if j > 0:
            pl.when(z == j)(functools.partial(take, 0, j))
        if j < layers - 1:
            pl.when(z == j)(functools.partial(take, 1, j))

    raw_a = sum_a[z] * adapter_scale
    raw_b = sum_b[z] * adapter_scale
    squares = jnp.sum(raw_a * raw_a) + jnp.sum(raw_b * raw_b)
    norm_buf[0] = jnp.full(norm_buf.shape[1:], squares, f32)

    def share(first, count, target):
        copies = []
        for k in range(1, count):
            at = first + k
            copies.append(
                copy_to(
                    norm_buf.at[first], norm_buf.at[at], norm_send.at[at], norm_recv.at[at], target(k)
                )
            )
            copies[-1].start()
        total = norm_buf[first]
        for k, c in enumerate(copies):
            c.wait()
            total = total + norm_buf[first + 1 + k]
        return total

    norm_buf[plane] = share(0, plane, in_plane)
    norm = jnp.sqrt(share(plane, layers, in_column)[0:1, 0:1])
    factor = jnp.minimum(f32(1.0), f32(limit) / (norm + f32(1e-06)))
    out_a[...] = (sum_a[z] * adapter_scale * factor).astype(bf16)
    out_b[...] = (sum_b[z] * adapter_scale * factor).astype(bf16)

    for j in range(layers):
        for a in range(2):
            to_twin(j, a).wait_send()
        for way in range(2):
            if (way == 0 and j > 0) or (way == 1 and j < layers - 1):

                def settle(way=way, j=j):
                    for a in range(2):
                        hop(way, j, a).wait_send()

                pl.when(moves(way, j))(settle)


def gather_line(layers, down, up, x, dy, w):
    cols, hidden = down.shape
    width = up.shape[1]
    sems = 4 * (layers - 1)
    anywhere = pl.BlockSpec(memory_space=pl.ANY)
    vmem = pl.BlockSpec(memory_space=pltpu.VMEM)
    return pl.pallas_call(
        functools.partial(gather_kernel, layers),
        out_shape=(
            jax.ShapeDtypeStruct((layers, 2, cols, hidden), bf16),
            jax.ShapeDtypeStruct((layers, 2, cols, width), bf16),
            jax.ShapeDtypeStruct(dy.shape, f32),
            jax.ShapeDtypeStruct(x.shape, f32),
            jax.ShapeDtypeStruct(x.shape, bf16),
            jax.ShapeDtypeStruct(dy.shape, bf16),
        ),
        in_specs=[anywhere, anywhere, vmem, vmem, anywhere],
        out_specs=[anywhere, anywhere, vmem, vmem, anywhere, anywhere],
        scratch_shapes=[
            pltpu.VMEM(w.shape, bf16),
            pltpu.SemaphoreType.DMA,
            pltpu.SemaphoreType.DMA((2,)),
            pltpu.SemaphoreType.DMA((2,)),
            pltpu.SemaphoreType.DMA((2,)),
            pltpu.SemaphoreType.DMA((sems,)),
            pltpu.SemaphoreType.DMA((sems,)),
            pltpu.SemaphoreType.DMA((sems + 2,)),
            pltpu.SemaphoreType.DMA((sems + 2,)),
        ],
        cost_estimate=pl.CostEstimate(flops=0, bytes_accessed=100_000_000, transcendentals=0),
        compiler_params=pltpu.CompilerParams(
            collective_id=0, has_side_effects=True, vmem_limit_bytes=40 * 2**20
        ),
    )(down, up, x, dy, w)


def reduce_line(layers, limit, part_a, part_b):
    _, _, cols, hidden = part_a.shape
    width = part_b.shape[3]
    vmem = pl.BlockSpec(memory_space=pltpu.VMEM)

    def both(lead, dtype):
        return [pltpu.VMEM((*lead, cols, m), dtype) for m in (hidden, width)]

    return pl.pallas_call(
        functools.partial(reduce_kernel, layers, limit),
        out_shape=(
            jax.ShapeDtypeStruct((cols, hidden), bf16),
            jax.ShapeDtypeStruct((cols, width), bf16),
        ),
        in_specs=[vmem] * 2,
        out_specs=[vmem] * 2,
        scratch_shapes=[
            *both((layers,), bf16),
            *both((layers,), f32),
            *both((2, layers), bf16),
            *both((2, layers), bf16),
            pltpu.VMEM((plane + layers, 8, 128), f32),
            pltpu.SemaphoreType.DMA((2 * layers,)),
            pltpu.SemaphoreType.DMA((2 * layers,)),
            pltpu.SemaphoreType.DMA((4 * layers,)),
            pltpu.SemaphoreType.DMA((4 * layers,)),
            pltpu.SemaphoreType.DMA((plane + layers,)),
            pltpu.SemaphoreType.DMA((plane + layers,)),
        ],
        cost_estimate=pl.CostEstimate(flops=0, bytes_accessed=100_000_000, transcendentals=0),
        compiler_params=pltpu.CompilerParams(
            collective_id=1, has_side_effects=True, vmem_limit_bytes=48 * 2**20
        ),
    )(part_a, part_b)


def short_line(x, dy, w, down_f, up_f, owner, slot):
    n = lax.axis_size("dev")
    me = lax.axis_index("dev")
    layers = n // plane
    tenants, hidden, rank = down_f.shape
    width = up_f.shape[2]
    cols = tenants * rank
    to_line = [(i, i ^ 2) for i in range(n)]

    def swap_line(v):
        return lax.ppermute(v, "dev", to_line)

    ids = (owner[:, 0] * tenants + slot).reshape(-1, 1)
    ids_p = swap_line(ids)
    downs, ups, frozen_y, frozen_dx, x_p, dy_p = gather_line(
        layers,
        jnp.transpose(down_f, (0, 2, 1)).reshape(cols, hidden),
        up_f.reshape(cols, width),
        x,
        dy,
        w,
    )
    downs = downs.reshape(layers * 2 * cols, hidden)
    ups = ups.reshape(layers * 2 * cols, width)

    col = jnp.arange(layers * 2 * cols, dtype=jnp.int32)[None, :]
    device = (col // (2 * cols)) * plane + (me % plane) // 2 * 2 + (col // cols) % 2
    label = device * tenants + (col // rank) % tenants

    def masked(v, i):
        return jnp.where(i == label, v, 0.0).astype(bf16)

    back_p = masked(dot_nt(dy_p, ups), ids_p)
    far_dx = swap_line((adapter_scale * dot_nn(back_p, downs)).astype(bf16))
    proj_p = masked(dot_nt(x_p, downs), ids_p)
    far_y = swap_line((adapter_scale * dot_nn(proj_p, ups)).astype(bf16))
    back = masked(dot_nt(dy, ups), ids)
    proj = masked(dot_nt(x, downs), ids)
    part_a = (dot_tn(back, x) + dot_tn(back_p, x_p)).astype(bf16)
    part_b = (dot_tn(proj, dy) + dot_tn(proj_p, dy_p)).astype(bf16)
    near_dx = (adapter_scale * dot_nn(back, downs)).astype(bf16)
    near_y = (adapter_scale * dot_nn(proj, ups)).astype(bf16)
    limit = float(tenants * n * rank * (hidden + width)) ** 0.5
    grad_a, grad_b = reduce_line(
        layers,
        limit,
        part_a.reshape(layers, 2, cols, hidden),
        part_b.reshape(layers, 2, cols, width),
    )
    layer_out = (frozen_y + (near_y.astype(f32) + far_y.astype(f32))).astype(bf16)
    grad_tokens = (frozen_dx + (near_dx.astype(f32) + far_dx.astype(f32))).astype(bf16)
    grad_a = jnp.transpose(grad_a.reshape(tenants, rank, hidden), (0, 2, 1))
    return (layer_out, grad_tokens, grad_a, grad_b.reshape(tenants, rank, width))


def local(*args):
    if lax.axis_size("dev") // plane <= 4:
        return short_line(*args)
    return long_line(*args)


def solution(mesh):
    rows = P(("groups", "dev"), None)
    stack = P(("groups", "dev"), None, None)
    return jax.shard_map(
        local,
        mesh=mesh,
        in_specs=(rows, rows, P(), stack, stack, rows, P(("groups", "dev"))),
        out_specs=(rows, rows, stack, stack),
        check_vma=False,
    )
```
